32 devices in a mesh: members: 2 (over x), tm: 16 (over z, y, core).
Axes of the slice: x: 2, y: 2, z: 4, core: 2. Of those that a mesh axis runs over, the one named last changes fastest.
Arguments:
- footprint: bfloat16 [8192, 128, 128], P(('members', 'tm')), parts along dimension 0, may hold values from -0.25 to 0.25
- block_row: int32 [32, 256], P(('members', 'tm')), parts along dimension 0, may hold values from 0 to 63
- block_col: int32 [32, 256], P(('members', 'tm')), parts along dimension 0, may hold values from 0 to 16383, as said below
- block_count: int32 [32], P(('members', 'tm')), parts along dimension 0, may hold values from 42 to 256, as said below
- observed_count: int32 [32], P(('members', 'tm')), parts along dimension 0, may hold values from 4096 to 8192, as said below
- emission: bfloat16 [32768, 128], P(('members', 'tm')), parts along dimension 0, may hold values from -6 to 6
- observed: float32 [2048, 128], P(('members', 'tm')), parts along dimension 0, may hold values from -6 to 6
- error_weight: float32 [2048, 128], P(('members', 'tm')), parts along dimension 0, may hold values from 0.25 to 4
- prior_precision: float32 [32768, 128], P(('members', 'tm')), parts along dimension 0, may hold values from 0.1 to 1
Outputs:
- gradient: float32 [32768, 128], P(('members', 'tm')), parts along dimension 0
- weighted_residual: float32 [2048, 128], P(('members', 'tm')), parts along dimension 0
The draws below stay inside these ranges and needn't reach their ends.
There are 2 independent parts, one for each index of `members`. The reference program is written for one: setup_inputs(seed, part) draws one part's arguments, and reference() takes and returns one part's arrays. A program takes and returns all parts, laid end to end along the dimension named above; each array names one. Nothing has to cross between parts.
Inputs may be any that keep to these rules, and one draw needn't show every extreme that they name: The first block_count[s] slots of shard s are live, the rest are padding; some shard has all 256 slots live. `block_col`: among the live slots of one shard at most 16 name cell blocks of one region panel (1024 consecutive cell blocks); some panel receives exactly 16 from every shard. `observed_count`: some shard has all its observations valid.
All inputs are finite; a program needn't handle non-finite values.
Results may differ from the reference program's by a relative error of at most 0.0015.
Values may be sent and summed in bfloat16 or wider, within the bound.
A program may use at most 128 MiB of HBM per device.

```python
import math
import jax
import jax.numpy as jnp
from jax import lax

BS = 128
CAP = 16
OB_DEV = 64
CB_DEV = 1024
NNZ_DEV = 256
OBS_BLOCKS = 1024
CELL_BLOCKS = 16384
N_TM = 16


def block_layout(key):
    counts = jax.random.randint(jax.random.fold_in(key, 11), (N_TM,), NNZ_DEV // 6, NNZ_DEV // 2 + 1)
    fullest = jax.random.randint(jax.random.fold_in(key, 12), (), 0, N_TM)
    counts = jnp.where(jnp.arange(N_TM) == fullest, NNZ_DEV, counts).astype(jnp.int32)
    hottest = jax.random.randint(jax.random.fold_in(key, 13), (), 0, N_TM)
    slot_index = jnp.arange(NNZ_DEV)
    spread = jnp.maximum(slot_index - CAP, 0) % (N_TM - 1)
    others = spread + (spread >= hottest).astype(jnp.int32)
    base_owner = jnp.where(slot_index < CAP, hottest, others)
    scores = jax.random.randint(jax.random.fold_in(key, 14), (N_TM, NNZ_DEV), 0, 2 ** 20)
    scores = jnp.where(slot_index[None, :] < counts[:, None], scores, 2 ** 21 + slot_index[None, :])
    order = jnp.argsort(scores, axis=1, stable=True)
    owners = base_owner[order]
    local_block = jax.random.randint(jax.random.fold_in(key, 15), (N_TM, NNZ_DEV), 0, CB_DEV)
    return (counts, (owners * CB_DEV + local_block).astype(jnp.int32))


def draw_block_count(key, part):
    return block_layout(key)[0]


def draw_block_col(key, part):
    return block_layout(key)[1]


def draw_observed_count(key, part):
    counts = jax.random.randint(jax.random.fold_in(key, 21), (N_TM,), OB_DEV * BS // 2, OB_DEV * BS + 1)
    fullest = jax.random.randint(jax.random.fold_in(key, 22), (), 0, N_TM)
    return jnp.where(jnp.arange(N_TM) == fullest, OB_DEV * BS, counts).astype(jnp.int32)


def place_ends(entries, own_key, low, high):
    dims = entries.shape
    spot = [jax.random.randint(jax.random.fold_in(own_key, axis), (), 0, dims[axis]) for axis in range(len(dims))]
    entries = entries.at[tuple(spot)].set(low)
    longest = dims.index(max(dims))
    spot[longest] = (spot[longest] + 1) % dims[longest]
    return entries.at[tuple(spot)].set(high)


def block_levels(stream_key, extent, pieces, smallest, largest):
    gain, own = 1.0, jax.random.fold_in(stream_key, 6)
    for axis_at, blocks in pieces:
        steps = jnp.exp(jax.random.uniform(jax.random.fold_in(own, axis_at), (blocks,), jnp.float32, smallest / len(pieces), largest / len(pieces)))
        gain = gain * jnp.repeat(steps, extent[axis_at] // blocks).reshape([-1 if axis == axis_at else 1 for axis in range(len(extent))])
    return gain


def scatter_about(rng, extent, scale, bound, pieces=(), kind=jnp.bfloat16):
    factor_of = block_levels(rng, extent, pieces, -0.22, 0.18) if pieces else 1.0
    entries = jax.random.normal(rng, extent, jnp.float32) * scale * factor_of
    return jnp.minimum(jnp.maximum(entries, -bound), bound).astype(kind)


def setup_inputs(seed: int = 0, part: int = 0) -> dict:
    keys = jax.random.split(jax.random.key(seed), 10)
    part_splits = jax.random.split(jax.random.fold_in(keys[9], part), 10)
    footprint = scatter_about(part_splits[0], (N_TM * NNZ_DEV, BS, BS), (BS * 4) ** -0.5, 0.25, ((0, 16),))
    block_row = place_ends(jax.random.randint(part_splits[1], (N_TM, NNZ_DEV), 0, OB_DEV), jax.random.fold_in(part_splits[1], 1), 0, OB_DEV - 1).astype(jnp.int32)
    block_col = draw_block_col(jax.random.fold_in(jax.random.fold_in(keys[9], part), 71), part)
    block_count = draw_block_count(jax.random.fold_in(jax.random.fold_in(keys[9], part), 71), part)
    observed_count = draw_observed_count(jax.random.fold_in(jax.random.fold_in(keys[9], part), 71), part)
    emission = scatter_about(part_splits[5], (CELL_BLOCKS, BS), 1.0, 6.0, ((0, 16),))
    observed = scatter_about(part_splits[6], (OBS_BLOCKS, BS), 1.0, 6.0, ((0, 16),), jnp.float32)
    error_weight = jnp.clip(jnp.exp(math.log(4.0) - 2.7725887 * jax.random.uniform(part_splits[7], (OBS_BLOCKS, BS), jnp.float32) ** block_levels(part_splits[7], (OBS_BLOCKS, BS), ((0, 16),), -0.2, 0.2)), 0.25, 4.0)
    prior_precision = jnp.clip(jnp.exp(math.log(1.0) - 2.3025851 * jax.random.uniform(part_splits[8], (CELL_BLOCKS, BS), jnp.float32) ** block_levels(part_splits[8], (CELL_BLOCKS, BS), ((0, 16),), -0.2, 0.2)), 0.1, 1.0)
    return dict(footprint=footprint, block_row=block_row, block_col=block_col, block_count=block_count, observed_count=observed_count, emission=emission, observed=observed, error_weight=error_weight, prior_precision=prior_precision)


def reference(footprint, block_row, block_col, block_count, observed_count, emission, observed, error_weight, prior_precision):
    slot_total = block_row.shape[1]
    foot_blocks = footprint.reshape(N_TM, slot_total, BS, BS)
    live_mask = jnp.arange(slot_total)[None, :] < block_count[:, None]
    state_rows = emission[block_col]

    def forward(carry, item):
        blocks, state_part, obs_block, keep_mask = item
        products = jnp.einsum('kij,kj->ki', blocks.astype(jnp.float32), state_part.astype(jnp.float32))
        products = jnp.where(keep_mask[:, None], products, 0.0)
        return carry, jax.ops.segment_sum(products, obs_block, num_segments=OB_DEV)

    _, obs_image = lax.scan(forward, jnp.zeros((), jnp.float32), (foot_blocks, state_rows, block_row, live_mask))
    obs_slot = jnp.arange(OB_DEV * BS).reshape(OB_DEV, BS)
    valid_mask = obs_slot[None, :, :] < observed_count[:, None, None]
    misfit = error_weight.reshape(N_TM, OB_DEV, BS) * (obs_image - observed.reshape(N_TM, OB_DEV, BS))
    weighted = jnp.where(valid_mask, misfit, 0.0).reshape(N_TM * OB_DEV, BS)
    rounded = weighted.astype(jnp.bfloat16)
    global_row = (jnp.arange(N_TM)[:, None] * OB_DEV + block_row).astype(jnp.int32)
    residual_rows = rounded[global_row]

    def adjoint(total, item):
        blocks, residual_part, cell_block, keep_mask = item
        products = jnp.einsum('kij,ki->kj', blocks.astype(jnp.float32), residual_part.astype(jnp.float32))
        products = jnp.where(keep_mask[:, None], products, 0.0)
        return total + jax.ops.segment_sum(products, cell_block, num_segments=N_TM * CB_DEV), None

    summed, _ = lax.scan(adjoint, jnp.zeros((N_TM * CB_DEV, BS), jnp.float32), (foot_blocks, residual_rows, block_col, live_mask))
    gradient = summed + prior_precision * emission.astype(jnp.float32)
    return gradient, weighted
```

```python
import functools

import jax
import jax.numpy as jnp
from jax import lax
from jax.experimental import pallas as pl
from jax.experimental.pallas import tpu as pltpu
from jax.sharding import PartitionSpec as P

CAP = 16
GROUP = 8
CHUNKS = 8
MESH = pl.DeviceIdType.MESH
BF16 = jnp.bfloat16
F32 = jnp.float32
I32 = jnp.int32


def iota(shape, dim):
    return lax.broadcasted_iota(I32, shape, dim)


def nn(a, b):
    return lax.dot_general(a, b, (((1,), (0,)), ((), ())), preferred_element_type=F32)


def nt(a, b):
    return lax.dot_general(a, b, (((1,), (1,)), ((), ())), preferred_element_type=F32)


def to_column(row):
    m = row.shape[1]
    diagonal = iota((m, m), 0) == iota((m, m), 1)
    return jnp.sum(jnp.where(diagonal, row.astype(F32), 0.0), axis=1, keepdims=True).astype(I32)


def one_hot(mask):
    return jnp.where(mask, 1.0, 0.0).astype(BF16)


def split(value):
    high = value.astype(BF16)
    low = (value - high.astype(F32)).astype(BF16)
    return high, low


def kernel(
    n,
    foot_hbm,
    row_ref,
    col_ref,
    count_ref,
    valid_ref,
    emission_hbm,
    observed_hbm,
    weight_hbm,
    prior_hbm,
    gradient_ref,
    weighted_ref,
    foot,
    emission,
    observed,
    weight,
    prior,
    ask_send,
    ask_recv,
    x_send,
    x_recv,
    p_send,
    p_recv,
    state,
    image_rows,
    residual,
    partial,
    foot_sem,
    in_sem,
    ask_ssem,
    ask_rsem,
    x_ssem,
    x_rsem,
    p_ssem,
    p_rsem,
):
    me = lax.axis_index("tm")
    slots = foot.shape[0]
    width = foot.shape[1]
    panel = emission.shape[0]
    obs_blocks = observed.shape[0]
    places = n * CAP

    emission_copy = pltpu.make_async_copy(emission_hbm, emission, in_sem.at[0])
    observed_copy = pltpu.make_async_copy(observed_hbm, observed, in_sem.at[1])
    weight_copy = pltpu.make_async_copy(weight_hbm, weight, in_sem.at[2])
    prior_copy = pltpu.make_async_copy(prior_hbm, prior, in_sem.at[3])
    chunk = slots // CHUNKS
    foot_copies = [
        pltpu.make_async_copy(
            foot_hbm.at[pl.ds(c * chunk, chunk)], foot.at[pl.ds(c * chunk, chunk)], foot_sem.at[c]
        )
        for c in range(CHUNKS)
    ]
    emission_copy.start()
    barrier = pltpu.get_barrier_semaphore()

    @pl.loop(1, n)
    def _(d):
        pl.semaphore_signal(
            barrier, inc=1, device_id={"tm": lax.rem(me + d, n)}, device_id_type=MESH
        )

    for copy in foot_copies:
        copy.start()
    observed_copy.start()
    weight_copy.start()
    prior_copy.start()

    col = col_ref[...]
    live = iota((1, slots), 1) < count_ref[0]
    owner = lax.div(col, panel)
    local = col - owner * panel
    mine = (owner == iota((n, slots), 0)) & live
    before = one_hot(iota((slots, slots), 0) < iota((slots, slots), 1))
    rank_of = nn(one_hot(mine), before)
    rank = jnp.sum(jnp.where(mine, rank_of, 0.0), axis=0, keepdims=True).astype(I32)
    place = jnp.where(live, owner * CAP + rank, -1)

    wanted = local + 1
    high = lax.div(wanted, 32)
    low = wanted - high * 32
    asked = jnp.concatenate(
        [
            jnp.where(mine, high.astype(F32), 0.0),
            jnp.where(mine, low.astype(F32), 0.0),
        ],
        axis=0,
    ).astype(BF16)
    lane = jnp.where(live, me * CAP + rank, -1)
    spread = nt(asked, one_hot(iota((places, slots), 0) == lane))
    asks = spread[:n] * 32.0 + spread[n:]
    for p in range(n):
        ask_send[p] = asks[p : p + 1]
    ask_recv[me] = ask_send[me]

    pl.semaphore_wait(barrier, n - 1)

    def exchange(send, recv, ssem, rsem, view):
        def copy_to(d):
            peer = lax.rem(me + d, n)
            return pltpu.make_async_remote_copy(
                src_ref=view(send, peer),
                dst_ref=view(recv, me),
                send_sem=ssem.at[peer],
                recv_sem=rsem.at[me],
                device_id={"tm": peer},
                device_id_type=MESH,
            )

        def copy_from(d):
            peer = lax.rem(me + d, n)
            return pltpu.make_async_remote_copy(
                src_ref=view(send, peer),
                dst_ref=view(recv, peer),
                send_sem=ssem.at[peer],
                recv_sem=rsem.at[peer],
                device_id={"tm": peer},
                device_id_type=MESH,
            )

        def start():
            @pl.loop(1, n)
            def _(d):
                copy_to(d).start()

        def wait_recv():
            @pl.loop(1, n)
            def _(d):
                copy_from(d).wait_recv()

        def wait_send():
            @pl.loop(1, n)
            def _(d):
                copy_to(d).wait_send()

        return start, wait_recv, wait_send

    def one(ref, index):
        return ref.at[index]

    def rows(ref, index):
        return ref.at[pl.ds(pl.multiple_of(index * CAP, CAP), CAP)]

    own = pl.ds(pl.multiple_of(me * CAP, CAP), CAP)

    ask_start, ask_wait, ask_done = exchange(ask_send, ask_recv, ask_ssem, ask_rsem, one)
    x_start, x_wait, x_done = exchange(x_send, x_recv, x_ssem, x_rsem, rows)
    p_start, p_wait, p_done = exchange(p_send, p_recv, p_ssem, p_rsem, rows)

    ask_start()
    place_column = to_column(place)
    to_slot = one_hot(place_column == iota((slots, places), 1))
    obs_row = jnp.where(live, row_ref[...], -1)
    obs_column = to_column(obs_row)
    emission_copy.wait()
    ask_wait()

    total = jnp.sum(ask_recv[...], axis=0).astype(I32)
    picked = nn(one_hot(to_column(total) == iota((places, panel), 1) + 1), emission[...])
    x_send[...] = picked.astype(BF16)
    x_recv[own] = x_send[own]
    x_start()

    for copy in foot_copies:
        copy.wait()
    observed_copy.wait()
    weight_copy.wait()
    x_wait()

    state[...] = nn(to_slot, x_recv[...])

    sub = iota((GROUP, width), 0)

    @pl.loop(0, slots // GROUP, unroll=8)
    def _(g):
        at = pl.ds(pl.multiple_of(g * GROUP, GROUP), GROUP)
        blocks = foot[at].reshape(GROUP * width, width)
        product = nt(state[at].astype(BF16), blocks)
        out = jnp.zeros((GROUP, width), F32)
        for k in range(GROUP):
            out = jnp.where(sub == k, product[:, k * width : (k + 1) * width], out)
        image_rows[at] = out

    to_obs = one_hot(obs_row == iota((obs_blocks, slots), 0))
    rows_value = image_rows[...]
    high, low = split(rows_value)
    image = nn(to_obs, high) + nn(to_obs, low)
    obs_slot = iota((obs_blocks, width), 0) * width + iota((obs_blocks, width), 1)
    misfit = jnp.where(obs_slot < valid_ref[0], weight[...] * (image - observed[...]), 0.0)
    weighted_ref[...] = misfit
    residual[...] = nn(one_hot(obs_column == iota((slots, obs_blocks), 1)), misfit.astype(BF16))

    @pl.loop(0, slots // GROUP, unroll=8)
    def _(g):
        at = pl.ds(pl.multiple_of(g * GROUP, GROUP), GROUP)
        blocks = foot[at].reshape(GROUP * width, width)
        value = residual[at]
        spread_out = jnp.concatenate(
            [jnp.where(sub == k, value, 0.0) for k in range(GROUP)], axis=1
        ).astype(BF16)
        partial[at] = nn(spread_out, blocks)

    high, low = split(partial[...])
    to_place = one_hot(iota((places, slots), 0) == place)
    p_send[:, :width] = nn(to_place, high).astype(BF16)
    p_send[:, width:] = nn(to_place, low).astype(BF16)
    p_recv[own] = p_send[own]
    p_start()
    scatter = one_hot(iota((panel, places), 0) + 1 == total)
    prior_copy.wait()
    ask_done()
    x_done()
    p_wait()
    summed = nn(scatter, p_recv[...])
    gradient_ref[...] = (
        summed[:, :width] + summed[:, width:] + prior[...] * emission[...].astype(F32)
    )
    p_done()


def on_device(
    footprint,
    block_row,
    block_col,
    block_count,
    observed_count,
    emission,
    observed,
    error_weight,
    prior_precision,
):
    n = lax.axis_size("tm")
    slots, width, _ = footprint.shape
    panel = emission.shape[0]
    obs_blocks = observed.shape[0]
    places = n * CAP
    any_spec = pl.BlockSpec(memory_space=pl.ANY)
    vmem_spec = pl.BlockSpec(memory_space=pltpu.VMEM)
    smem_spec = pl.BlockSpec(memory_space=pltpu.SMEM)
    dma = pltpu.SemaphoreType.DMA
    return pl.pallas_call(
        functools.partial(kernel, n),
        out_shape=(
            jax.ShapeDtypeStruct((panel, width), F32),
            jax.ShapeDtypeStruct((obs_blocks, width), F32),
        ),
        in_specs=[
            any_spec,
            vmem_spec,
            vmem_spec,
            smem_spec,
            smem_spec,
            any_spec,
            any_spec,
            any_spec,
            any_spec,
        ],
        out_specs=(vmem_spec, vmem_spec),
        scratch_shapes=[
            pltpu.VMEM((slots, width, width), BF16),
            pltpu.VMEM((panel, width), BF16),
            pltpu.VMEM((obs_blocks, width), F32),
            pltpu.VMEM((obs_blocks, width), F32),
            pltpu.VMEM((panel, width), F32),
            pltpu.VMEM((n, 1, places), F32),
            pltpu.VMEM((n, 1, places), F32),
            pltpu.VMEM((places, width), BF16),
            pltpu.VMEM((places, width), BF16),
            pltpu.VMEM((places, 2 * width), BF16),
            pltpu.VMEM((places, 2 * width), BF16),
            pltpu.VMEM((slots, width), F32),
            pltpu.VMEM((slots, width), F32),
            pltpu.VMEM((slots, width), F32),
            pltpu.VMEM((slots, width), F32),
            dma((CHUNKS,)),
            dma((4,)),
            dma((n,)),
            dma((n,)),
            dma((n,)),
            dma((n,)),
            dma((n,)),
            dma((n,)),
        ],
        compiler_params=pltpu.CompilerParams(
            collective_id=0, has_side_effects=True, vmem_limit_bytes=48 * 1024 * 1024
        ),
        cost_estimate=pl.CostEstimate(
            flops=4 * slots * width * width,
            bytes_accessed=footprint.size * 2 + panel * width * 10,
            transcendentals=0,
        ),
    )(
        footprint,
        block_row,
        block_col,
        block_count,
        observed_count,
        emission,
        observed,
        error_weight,
        prior_precision,
    )


def solution(mesh):
    placed = (
        P(("members", "tm"), None, None),
        P(("members", "tm"), None),
        P(("members", "tm"), None),
        P(("members", "tm")),
        P(("members", "tm")),
        P(("members", "tm"), None),
        P(("members", "tm"), None),
        P(("members", "tm"), None),
        P(("members", "tm"), None),
    )
    return jax.shard_map(
        on_device,
        mesh=mesh,
        in_specs=placed,
        out_specs=(P(("members", "tm"), None), P(("members", "tm"), None)),
        check_vma=False,
    )
```

```python
import functools

import jax
import jax.numpy as jnp
from jax import lax
from jax.experimental import pallas as pl
from jax.experimental.pallas import tpu as pltpu
from jax.sharding import PartitionSpec as P

CAP = 16
GROUP = 8
CHUNKS = 8
MESH = pl.DeviceIdType.MESH
BF16 = jnp.bfloat16
F32 = jnp.float32
I32 = jnp.int32


def iota(shape, dim):
    return lax.broadcasted_iota(I32, shape, dim)


def nn(a, b):
    return lax.dot_general(a, b, (((1,), (0,)), ((), ())), preferred_element_type=F32)


def nt(a, b):
    return lax.dot_general(a, b, (((1,), (1,)), ((), ())), preferred_element_type=F32)


def to_column(row):
    m = row.shape[1]
    diagonal = iota((m, m), 0) == iota((m, m), 1)
    return jnp.sum(jnp.where(diagonal, row.astype(F32), 0.0), axis=1, keepdims=True).astype(I32)


def one_hot(mask):
    return jnp.where(mask, 1.0, 0.0).astype(BF16)


def split(value):
    high = value.astype(BF16)
    low = (value - high.astype(F32)).astype(BF16)
    return high, low


def kernel(
    n,
    foot_hbm,
    row_hbm,
    col_hbm,
    count_hbm,
    valid_hbm,
    emission_hbm,
    observed_hbm,
    weight_hbm,
    prior_hbm,
    gradient_ref,
    weighted_ref,
    row_ref,
    col_ref,
    count_ref,
    valid_ref,
    foot,
    emission,
    observed,
    weight,
    prior,
    ask_send,
    ask_recv,
    x_send,
    x_recv,
    p_send,
    p_recv,
    state,
    image_rows,
    residual,
    partial,
    foot_sem,
    in_sem,
    ask_ssem,
    ask_rsem,
    x_ssem,
    x_rsem,
    p_ssem,
    p_rsem,
):
    me = lax.axis_index("tm")
    slots = foot.shape[0]
    width = foot.shape[1]
    panel = emission.shape[0]
    obs_blocks = observed.shape[0]
    places = n * CAP

    col_copy = pltpu.make_async_copy(col_hbm, col_ref, in_sem.at[4])
    count_copy = pltpu.make_async_copy(count_hbm, count_ref, in_sem.at[5])
    row_copy = pltpu.make_async_copy(row_hbm, row_ref, in_sem.at[6])
    valid_copy = pltpu.make_async_copy(valid_hbm, valid_ref, in_sem.at[7])
    col_copy.start()
    count_copy.start()
    emission_copy = pltpu.make_async_copy(emission_hbm, emission, in_sem.at[0])
    observed_copy = pltpu.make_async_copy(observed_hbm, observed, in_sem.at[1])
    weight_copy = pltpu.make_async_copy(weight_hbm, weight, in_sem.at[2])
    prior_copy = pltpu.make_async_copy(prior_hbm, prior, in_sem.at[3])
    chunk = slots // CHUNKS
    foot_copies = [
        pltpu.make_async_copy(
            foot_hbm.at[pl.ds(c * chunk, chunk)], foot.at[pl.ds(c * chunk, chunk)], foot_sem.at[c]
        )
        for c in range(CHUNKS)
    ]
    barrier = pltpu.get_barrier_semaphore()

    @pl.loop(1, n)
    def _(d):
        pl.semaphore_signal(
            barrier, inc=1, device_id={"tm": lax.rem(me + d, n)}, device_id_type=MESH
        )

    row_copy.start()
    emission_copy.start()
    valid_copy.start()
    for copy in foot_copies:
        copy.start()
    observed_copy.start()
    weight_copy.start()
    prior_copy.start()
    col_copy.wait()
    count_copy.wait()

    col = col_ref[...]
    live = iota((1, slots), 1) < count_ref[0]
    owner = lax.div(col, panel)
    local = col - owner * panel
    mine = (owner == iota((n, slots), 0)) & live
    before = one_hot(iota((slots, slots), 0) < iota((slots, slots), 1))
    rank_of = nn(one_hot(mine), before)
    rank = jnp.sum(jnp.where(mine, rank_of, 0.0), axis=0, keepdims=True).astype(I32)
    place = jnp.where(live, owner * CAP + rank, -1)

    wanted = local + 1
    high = lax.div(wanted, 32)
    low = wanted - high * 32
    asked = jnp.concatenate(
        [
            jnp.where(mine, high.astype(F32), 0.0),
            jnp.where(mine, low.astype(F32), 0.0),
        ],
        axis=0,
    ).astype(BF16)
    lane = jnp.where(live, me * CAP + rank, -1)
    spread = nt(asked, one_hot(iota((places, slots), 0) == lane))
    asks = spread[:n] * 32.0 + spread[n:]
    for p in range(n):
        ask_send[p] = asks[p : p + 1]
    ask_recv[me] = ask_send[me]

    pl.semaphore_wait(barrier, n - 1)

    def exchange(send, recv, ssem, rsem, view):
        def copy_to(d):
            peer = lax.rem(me + d, n)
            return pltpu.make_async_remote_copy(
                src_ref=view(send, peer),
                dst_ref=view(recv, me),
                send_sem=ssem.at[peer],
                recv_sem=rsem.at[me],
                device_id={"tm": peer},
                device_id_type=MESH,
            )

        def copy_from(d):
            peer = lax.rem(me - d + n, n)
            return pltpu.make_async_remote_copy(
                src_ref=view(send, peer),
                dst_ref=view(recv, peer),
                send_sem=ssem.at[peer],
                recv_sem=rsem.at[peer],
                device_id={"tm": peer},
                device_id_type=MESH,
            )

        def start():
            @pl.loop(1, n)
            def _(d):
                copy_to(d).start()

        def wait_recv():
            @pl.loop(1, n)
            def _(d):
                copy_from(d).wait_recv()

        def wait_send():
            @pl.loop(1, n)
            def _(d):
                copy_to(d).wait_send()

        return start, wait_recv, wait_send

    def one(ref, index):
        return ref.at[index]

    def rows(ref, index):
        return ref.at[pl.ds(pl.multiple_of(index * CAP, CAP), CAP)]

    own = pl.ds(pl.multiple_of(me * CAP, CAP), CAP)

    ask_start, ask_wait, ask_done = exchange(ask_send, ask_recv, ask_ssem, ask_rsem, one)
    x_start, x_wait, x_done = exchange(x_send, x_recv, x_ssem, x_rsem, rows)
    p_start, p_wait, p_done = exchange(p_send, p_recv, p_ssem, p_rsem, rows)

    ask_start()
    place_column = to_column(place)
    to_slot = one_hot(place_column == iota((slots, places), 1))
    row_copy.wait()
    obs_row = jnp.where(live, row_ref[...], -1)
    obs_column = to_column(obs_row)
    emission_copy.wait()
    ask_wait()

    total = jnp.sum(ask_recv[...], axis=0).astype(I32)
    picked = nn(one_hot(to_column(total) == iota((places, panel), 1) + 1), emission[...])
    x_send[...] = picked.astype(BF16)
    x_recv[own] = x_send[own]
    x_start()

    for copy in foot_copies:
        copy.wait()
    observed_copy.wait()
    weight_copy.wait()
    valid_copy.wait()
    x_wait()

    state[...] = nn(to_slot, x_recv[...])

    sub = iota((GROUP, width), 0)

    @pl.loop(0, slots // GROUP, unroll=32)
    def _(g):
        at = pl.ds(pl.multiple_of(g * GROUP, GROUP), GROUP)
        blocks = foot[at].reshape(GROUP * width, width)
        product = nt(state[at].astype(BF16), blocks)
        out = jnp.zeros((GROUP, width), F32)
        for k in range(GROUP):
            out = jnp.where(sub == k, product[:, k * width : (k + 1) * width], out)
        image_rows[at] = out

    to_obs = one_hot(obs_row == iota((obs_blocks, slots), 0))
    rows_value = image_rows[...]
    high, low = split(rows_value)
    image = nn(to_obs, high) + nn(to_obs, low)
    obs_slot = iota((obs_blocks, width), 0) * width + iota((obs_blocks, width), 1)
    misfit = jnp.where(obs_slot < valid_ref[0], weight[...] * (image - observed[...]), 0.0)
    weighted_ref[...] = misfit
    residual[...] = nn(one_hot(obs_column == iota((slots, obs_blocks), 1)), misfit.astype(BF16))

    @pl.loop(0, slots // GROUP, unroll=32)
    def _(g):
        at = pl.ds(pl.multiple_of(g * GROUP, GROUP), GROUP)
        blocks = foot[at].reshape(GROUP * width, width)
        value = residual[at]
        spread_out = jnp.concatenate(
            [jnp.where(sub == k, value, 0.0) for k in range(GROUP)], axis=1
        ).astype(BF16)
        partial[at] = nn(spread_out, blocks)

    high, low = split(partial[...])
    to_place = one_hot(iota((places, slots), 0) == place)
    p_send[:, :width] = nn(to_place, high).astype(BF16)
    p_send[:, width:] = nn(to_place, low).astype(BF16)
    p_recv[own] = p_send[own]
    p_start()
    scatter = one_hot(iota((panel, places), 0) + 1 == total)
    prior_copy.wait()
    ask_done()
    x_done()
    p_wait()
    summed = nn(scatter, p_recv[...])
    gradient_ref[...] = (
        summed[:, :width] + summed[:, width:] + prior[...] * emission[...].astype(F32)
    )
    p_done()


def in_hbm(value):
    return pltpu.with_memory_space_constraint(value, pltpu.HBM)


def on_device(
    footprint,
    block_row,
    block_col,
    block_count,
    observed_count,
    emission,
    observed,
    error_weight,
    prior_precision,
):
    n = lax.axis_size("tm")
    slots, width, _ = footprint.shape
    panel = emission.shape[0]
    obs_blocks = observed.shape[0]
    places = n * CAP
    hbm_spec = pl.BlockSpec(memory_space=pltpu.HBM)
    any_spec = pl.BlockSpec(memory_space=pl.ANY)
    vmem_spec = pl.BlockSpec(memory_space=pltpu.VMEM)
    dma = pltpu.SemaphoreType.DMA
    outs = (
        jax.ShapeDtypeStruct((panel, width), F32),
        jax.ShapeDtypeStruct((obs_blocks, width), F32),
    )
    results = pl.pallas_call(
        functools.partial(kernel, n),
        out_shape=outs,
        in_specs=[hbm_spec] * 9,
        out_specs=(vmem_spec, vmem_spec),
        scratch_shapes=[
            pltpu.VMEM((1, slots), I32),
            pltpu.VMEM((1, slots), I32),
            pltpu.SMEM((1,), I32),
            pltpu.SMEM((1,), I32),
            pltpu.VMEM((slots, width, width), BF16),
            pltpu.VMEM((panel, width), BF16),
            pltpu.VMEM((obs_blocks, width), F32),
            pltpu.VMEM((obs_blocks, width), F32),
            pltpu.VMEM((panel, width), F32),
            pltpu.VMEM((n, 1, places), F32),
            pltpu.VMEM((n, 1, places), F32),
            pltpu.VMEM((places, width), BF16),
            pltpu.VMEM((places, width), BF16),
            pltpu.VMEM((places, 2 * width), BF16),
            pltpu.VMEM((places, 2 * width), BF16),
            pltpu.VMEM((slots, width), F32),
            pltpu.VMEM((slots, width), F32),
            pltpu.VMEM((slots, width), F32),
            pltpu.VMEM((slots, width), F32),
            dma((CHUNKS,)),
            dma((8,)),
            dma((n,)),
            dma((n,)),
            dma((n,)),
            dma((n,)),
            dma((n,)),
            dma((n,)),
        ],
        compiler_params=pltpu.CompilerParams(
            collective_id=0, has_side_effects=True, vmem_limit_bytes=48 * 1024 * 1024
        ),
        cost_estimate=pl.CostEstimate(
            flops=4 * slots * width * width,
            bytes_accessed=footprint.size * 2 + panel * width * 10,
            transcendentals=0,
        ),
    )(
        in_hbm(footprint),
        in_hbm(block_row),
        in_hbm(block_col),
        block_count,
        observed_count,
        in_hbm(emission),
        in_hbm(observed),
        in_hbm(error_weight),
        in_hbm(prior_precision),
    )
    return results


def solution(mesh):
    placed = (
        P(("members", "tm"), None, None),
        P(("members", "tm"), None),
        P(("members", "tm"), None),
        P(("members", "tm")),
        P(("members", "tm")),
        P(("members", "tm"), None),
        P(("members", "tm"), None),
        P(("members", "tm"), None),
        P(("members", "tm"), None),
    )
    return jax.shard_map(
        on_device,
        mesh=mesh,
        in_specs=placed,
        out_specs=(P(("members", "tm"), None), P(("members", "tm"), None)),
        check_vma=False,
    )
```

```python
import functools

import jax
import jax.numpy as jnp
from jax import lax
from jax.experimental import pallas as pl
from jax.experimental.pallas import tpu as pltpu
from jax.sharding import PartitionSpec as P

CAP = 16
BATCH = 4
CHUNKS = 8
MESH = pl.DeviceIdType.MESH
BF16 = jnp.bfloat16
F32 = jnp.float32
I32 = jnp.int32


def iota(shape, dim):
    return lax.broadcasted_iota(I32, shape, dim)


def nn(a, b):
    return lax.dot_general(a, b, (((1,), (0,)), ((), ())), preferred_element_type=F32)


def nt(a, b):
    return lax.dot_general(a, b, (((1,), (1,)), ((), ())), preferred_element_type=F32)


def to_column(row):
    m = row.shape[1]
    diagonal = iota((m, m), 0) == iota((m, m), 1)
    return jnp.sum(jnp.where(diagonal, row.astype(F32), 0.0), axis=1, keepdims=True).astype(I32)


def one_hot(mask):
    return jnp.where(mask, 1.0, 0.0).astype(BF16)


def split(value):
    high = value.astype(BF16)
    low = (value - high.astype(F32)).astype(BF16)
    return high, low


def kernel(
    n,
    foot_hbm,
    row_hbm,
    col_hbm,
    count_hbm,
    valid_hbm,
    emission_hbm,
    observed_hbm,
    weight_hbm,
    prior_hbm,
    gradient_ref,
    weighted_ref,
    row_ref,
    col_ref,
    count_ref,
    valid_ref,
    foot,
    emission,
    observed,
    weight,
    prior,
    ask_send,
    ask_recv,
    x_send,
    x_recv,
    p_send,
    p_recv,
    slot_row,
    slot_at,
    image_rows,
    residual,
    foot_sem,
    slot_sem,
    in_sem,
    ask_ssem,
    ask_rsem,
    x_ssem,
    x_rsem,
    p_ssem,
    p_rsem,
):
    me = lax.axis_index("tm")
    slots = foot.shape[0]
    width = foot.shape[1]
    panel = emission.shape[0]
    obs_blocks = observed.shape[0]
    places = n * CAP

    col_copy = pltpu.make_async_copy(col_hbm, col_ref, in_sem.at[4])
    count_copy = pltpu.make_async_copy(count_hbm, count_ref, in_sem.at[5])
    row_copy = pltpu.make_async_copy(row_hbm, row_ref, in_sem.at[6])
    valid_copy = pltpu.make_async_copy(valid_hbm, valid_ref, in_sem.at[7])
    col_copy.start()
    count_copy.start()
    emission_copy = pltpu.make_async_copy(emission_hbm, emission, in_sem.at[0])
    observed_copy = pltpu.make_async_copy(observed_hbm, observed, in_sem.at[1])
    weight_copy = pltpu.make_async_copy(weight_hbm, weight, in_sem.at[2])
    prior_copy = pltpu.make_async_copy(prior_hbm, prior, in_sem.at[3])
    chunk = slots // CHUNKS
    foot_copies = [
        pltpu.make_async_copy(
            foot_hbm.at[pl.ds(c * chunk, chunk)], foot.at[pl.ds(c * chunk, chunk)], foot_sem.at[c]
        )
        for c in range(CHUNKS)
    ]
    barrier = pltpu.get_barrier_semaphore()

    @pl.loop(1, n)
    def _(d):
        pl.semaphore_signal(
            barrier, inc=1, device_id={"tm": lax.rem(me + d, n)}, device_id_type=MESH
        )

    row_copy.start()
    emission_copy.start()
    valid_copy.start()
    for copy in foot_copies:
        copy.start()
    observed_copy.start()
    weight_copy.start()
    prior_copy.start()
    col_copy.wait()
    count_copy.wait()

    col = col_ref[...]
    live = iota((1, slots), 1) < count_ref[0]
    owner = lax.div(col, panel)
    local = col - owner * panel
    mine = (owner == iota((n, slots), 0)) & live
    before = one_hot(iota((slots, slots), 0) < iota((slots, slots), 1))
    rank_of = nn(one_hot(mine), before)
    rank = jnp.sum(jnp.where(mine, rank_of, 0.0), axis=0, keepdims=True).astype(I32)
    place = jnp.where(live, owner * CAP + rank, -1)

    wanted = local + 1
    high = lax.div(wanted, 32)
    low = wanted - high * 32
    asked = jnp.concatenate(
        [
            jnp.where(mine, high.astype(F32), 0.0),
            jnp.where(mine, low.astype(F32), 0.0),
        ],
        axis=0,
    ).astype(BF16)
    lane = jnp.where(live, me * CAP + rank, -1)
    spread = nt(asked, one_hot(iota((places, slots), 0) == lane))
    asks = spread[:n] * 32.0 + spread[n:]
    for p in range(n):
        ask_send[p] = asks[p : p + 1]
    ask_recv[me] = ask_send[me]

    pl.semaphore_wait(barrier, n - 1)

    def copy_to(exchange, d):
        send, recv, ssem, rsem, view = exchange
        peer = lax.rem(me + d, n)
        return pltpu.make_async_remote_copy(
            src_ref=view(send, peer),
            dst_ref=view(recv, me),
            send_sem=ssem.at[peer],
            recv_sem=rsem.at[me],
            device_id={"tm": peer},
            device_id_type=MESH,
        )

    def copy_from(exchange, d):
        send, recv, ssem, rsem, view = exchange
        peer = lax.rem(me - d + n, n)
        return pltpu.make_async_remote_copy(
            src_ref=view(send, peer),
            dst_ref=view(recv, peer),
            send_sem=ssem.at[peer],
            recv_sem=rsem.at[peer],
            device_id={"tm": peer},
            device_id_type=MESH,
        )

    def start(exchange):
        @pl.loop(1, n)
        def _(d):
            copy_to(exchange, d).start()

    def wait_recv(exchange):
        @pl.loop(1, n)
        def _(d):
            copy_from(exchange, d).wait_recv()

    def wait_send(exchange):
        @pl.loop(1, n)
        def _(d):
            copy_to(exchange, d).wait_send()

    def one(ref, index):
        return ref.at[index]

    def span(index):
        return pl.ds(pl.multiple_of(index * CAP, CAP), CAP)

    def rows(ref, index):
        return ref.at[span(index)]

    own = span(me)
    ask = (ask_send, ask_recv, ask_ssem, ask_rsem, one)
    x = (x_send, x_recv, x_ssem, x_rsem, rows)
    p = (p_send, p_recv, p_ssem, p_rsem, rows)

    start(ask)

    row_copy.wait()
    index = iota((1, slots), 1)
    high = lax.div(index, 32)
    fields = iota((CAP, slots), 0)
    fields = jnp.where(
        fields == 0,
        high,
        jnp.where(fields == 1, index - high * 32, jnp.where(fields == 2, row_ref[...] + 1, 0)),
    )
    moved = nt(fields.astype(F32).astype(BF16), one_hot(iota((places, slots), 0) == place))
    slot_row[...] = (moved[0:1] * 32.0 + moved[1:2]).astype(I32)
    slot_copy = pltpu.make_async_copy(slot_row, slot_at, slot_sem)
    slot_copy.start()
    obs_row = moved[2:3].astype(I32)
    obs_column = to_column(obs_row)
    to_obs = one_hot(obs_row == iota((obs_blocks, places), 0) + 1)
    from_obs = one_hot(obs_column == iota((places, obs_blocks), 1) + 1)
    emission_copy.wait()
    wait_recv(ask)

    total = jnp.sum(ask_recv[...], axis=0).astype(I32)
    picked = nn(one_hot(to_column(total) == iota((places, panel), 1) + 1), emission[...])
    x_send[...] = picked.astype(BF16)
    x_recv[own] = x_send[own]
    start(x)

    for copy in foot_copies:
        copy.wait()
    observed_copy.wait()
    weight_copy.wait()
    valid_copy.wait()
    slot_copy.wait()

    sub = iota((CAP, width), 0)

    def blocks_of(panel_index):
        first = panel_index * CAP
        indices = [jnp.clip(slot_at[0, first + k], 0, slots - 1) for k in range(CAP)]
        return jnp.concatenate([foot[index] for index in indices], axis=0)

    for d0 in range(0, n, BATCH):
        steps = range(d0, min(d0 + BATCH, n))
        for d in steps:
            if d > 0:
                copy_from(x, d).wait_recv()
        for d in steps:
            source = lax.rem(me - d + n, n)
            product = nt(x_recv[span(source)], blocks_of(source))
            out = jnp.zeros((CAP, width), F32)
            for k in range(CAP):
                out = jnp.where(sub == k, product[:, k * width : (k + 1) * width], out)
            image_rows[span(source)] = out

    rows_value = image_rows[...]
    high, low = split(rows_value)
    image = nn(to_obs, high) + nn(to_obs, low)
    obs_slot = iota((obs_blocks, width), 0) * width + iota((obs_blocks, width), 1)
    misfit = jnp.where(obs_slot < valid_ref[0], weight[...] * (image - observed[...]), 0.0)
    weighted_ref[...] = misfit
    residual[...] = nn(from_obs, misfit.astype(BF16)).astype(BF16)

    for d0 in range(1, n + 1, BATCH):
        steps = range(d0, min(d0 + BATCH, n + 1))
        for d in steps:
            target = lax.rem(me + d, n)
            value = residual[span(target)].astype(F32)
            wide = jnp.concatenate(
                [jnp.where(sub == k, value, 0.0) for k in range(CAP)], axis=1
            ).astype(BF16)
            high, low = split(nn(wide, blocks_of(target)))
            sink = p_send if d < n else p_recv
            sink[span(target), :width] = high
            sink[span(target), width:] = low
        for d in steps:
            if d < n:
                copy_to(p, d).start()
    scatter = one_hot(iota((panel, places), 0) + 1 == total)
    prior_copy.wait()
    wait_send(ask)
    wait_send(x)
    wait_recv(p)
    summed = nn(scatter, p_recv[...])
    gradient_ref[...] = (
        summed[:, :width] + summed[:, width:] + prior[...] * emission[...].astype(F32)
    )
    wait_send(p)


def in_hbm(value):
    return pltpu.with_memory_space_constraint(value, pltpu.HBM)


def on_device(
    footprint,
    block_row,
    block_col,
    block_count,
    observed_count,
    emission,
    observed,
    error_weight,
    prior_precision,
):
    n = lax.axis_size("tm")
    slots, width, _ = footprint.shape
    panel = emission.shape[0]
    obs_blocks = observed.shape[0]
    places = n * CAP
    hbm_spec = pl.BlockSpec(memory_space=pltpu.HBM)
    any_spec = pl.BlockSpec(memory_space=pl.ANY)
    vmem_spec = pl.BlockSpec(memory_space=pltpu.VMEM)
    dma = pltpu.SemaphoreType.DMA
    outs = (
        jax.ShapeDtypeStruct((panel, width), F32),
        jax.ShapeDtypeStruct((obs_blocks, width), F32),
    )
    results = pl.pallas_call(
        functools.partial(kernel, n),
        out_shape=outs,
        in_specs=[hbm_spec] * 9,
        out_specs=(vmem_spec, vmem_spec),
        scratch_shapes=[
            pltpu.VMEM((1, slots), I32),
            pltpu.VMEM((1, slots), I32),
            pltpu.SMEM((1,), I32),
            pltpu.SMEM((1,), I32),
            pltpu.VMEM((slots, width, width), BF16),
            pltpu.VMEM((panel, width), BF16),
            pltpu.VMEM((obs_blocks, width), F32),
            pltpu.VMEM((obs_blocks, width), F32),
            pltpu.VMEM((panel, width), F32),
            pltpu.VMEM((n, 1, places), F32),
            pltpu.VMEM((n, 1, places), F32),
            pltpu.VMEM((places, width), BF16),
            pltpu.VMEM((places, width), BF16),
            pltpu.VMEM((places, 2 * width), BF16),
            pltpu.VMEM((places, 2 * width), BF16),
            pltpu.VMEM((1, places), I32),
            pltpu.SMEM((1, places), I32),
            pltpu.VMEM((places, width), F32),
            pltpu.VMEM((places, width), BF16),
            dma((CHUNKS,)),
            dma(()),
            dma((8,)),
            dma((n,)),
            dma((n,)),
            dma((n,)),
            dma((n,)),
            dma((n,)),
            dma((n,)),
        ],
        compiler_params=pltpu.CompilerParams(
            collective_id=0, has_side_effects=True, vmem_limit_bytes=48 * 1024 * 1024
        ),
        cost_estimate=pl.CostEstimate(
            flops=4 * slots * width * width,
            bytes_accessed=footprint.size * 2 + panel * width * 10,
            transcendentals=0,
        ),
    )(
        in_hbm(footprint),
        in_hbm(block_row),
        in_hbm(block_col),
        block_count,
        observed_count,
        in_hbm(emission),
        in_hbm(observed),
        in_hbm(error_weight),
        in_hbm(prior_precision),
    )
    return results


def solution(mesh):
    placed = (
        P(("members", "tm"), None, None),
        P(("members", "tm"), None),
        P(("members", "tm"), None),
        P(("members", "tm")),
        P(("members", "tm")),
        P(("members", "tm"), None),
        P(("members", "tm"), None),
        P(("members", "tm"), None),
        P(("members", "tm"), None),
    )
    return jax.shard_map(
        on_device,
        mesh=mesh,
        in_specs=placed,
        out_specs=(P(("members", "tm"), None), P(("members", "tm"), None)),
        check_vma=False,
    )
```

```python
import functools

import jax
import jax.numpy as jnp
from jax import lax
from jax.experimental import pallas as pl
from jax.experimental.pallas import tpu as pltpu
from jax.sharding import PartitionSpec as P

CAP = 16
BATCH = 4
PARTS = 4
CHUNKS = 8
MESH = pl.DeviceIdType.MESH
BF16 = jnp.bfloat16
F32 = jnp.float32
I32 = jnp.int32


def iota(shape, dim):
    return lax.broadcasted_iota(I32, shape, dim)


def nn(a, b):
    return lax.dot_general(a, b, (((1,), (0,)), ((), ())), preferred_element_type=F32)


def nt(a, b):
    return lax.dot_general(a, b, (((1,), (1,)), ((), ())), preferred_element_type=F32)


def to_column(row):
    m = row.shape[1]
    diagonal = iota((m, m), 0) == iota((m, m), 1)
    return jnp.sum(jnp.where(diagonal, row.astype(F32), 0.0), axis=1, keepdims=True).astype(I32)


def one_hot(mask):
    return jnp.where(mask, 1.0, 0.0).astype(BF16)


def split(value):
    high = value.astype(BF16)
    low = (value - high.astype(F32)).astype(BF16)
    return high, low


def kernel(
    n,
    foot_hbm,
    row_hbm,
    col_hbm,
    count_hbm,
    valid_hbm,
    emission_hbm,
    observed_hbm,
    weight_hbm,
    prior_hbm,
    gradient_ref,
    weighted_ref,
    row_ref,
    col_ref,
    count_ref,
    valid_ref,
    foot,
    emission,
    observed,
    weight,
    prior,
    ask_send,
    ask_recv,
    x_send,
    x_recv,
    p_send,
    p_recv,
    slot_row,
    slot_at,
    image_rows,
    residual,
    foot_sem,
    slot_sem,
    in_sem,
    ask_ssem,
    ask_rsem,
    x_ssem,
    x_rsem,
    p_ssem,
    p_rsem,
):
    me = lax.axis_index("tm")
    slots = foot.shape[0]
    width = foot.shape[1]
    panel = emission.shape[0]
    obs_blocks = observed.shape[0]
    places = n * CAP

    col_copy = pltpu.make_async_copy(col_hbm, col_ref, in_sem.at[4])
    count_copy = pltpu.make_async_copy(count_hbm, count_ref, in_sem.at[5])
    row_copy = pltpu.make_async_copy(row_hbm, row_ref, in_sem.at[6])
    valid_copy = pltpu.make_async_copy(valid_hbm, valid_ref, in_sem.at[7])
    col_copy.start()
    count_copy.start()
    emission_copy = pltpu.make_async_copy(emission_hbm, emission, in_sem.at[0])
    observed_copy = pltpu.make_async_copy(observed_hbm, observed, in_sem.at[1])
    weight_copy = pltpu.make_async_copy(weight_hbm, weight, in_sem.at[2])
    prior_copy = pltpu.make_async_copy(prior_hbm, prior, in_sem.at[3])
    chunk = slots // CHUNKS
    foot_copies = [
        pltpu.make_async_copy(
            foot_hbm.at[pl.ds(c * chunk, chunk)], foot.at[pl.ds(c * chunk, chunk)], foot_sem.at[c]
        )
        for c in range(CHUNKS)
    ]
    barrier = pltpu.get_barrier_semaphore()

    @pl.loop(1, n)
    def _(d):
        pl.semaphore_signal(
            barrier, inc=1, device_id={"tm": lax.rem(me + d, n)}, device_id_type=MESH
        )

    row_copy.start()
    emission_copy.start()
    valid_copy.start()
    for copy in foot_copies:
        copy.start()
    observed_copy.start()
    weight_copy.start()
    prior_copy.start()
    col_copy.wait()
    count_copy.wait()

    col = col_ref[...]
    live = iota((1, slots), 1) < count_ref[0]
    owner = lax.div(col, panel)
    local = col - owner * panel
    mine = (owner == iota((n, slots), 0)) & live
    before = one_hot(iota((slots, slots), 0) < iota((slots, slots), 1))
    rank_of = nn(one_hot(mine), before)
    rank = jnp.sum(jnp.where(mine, rank_of, 0.0), axis=0, keepdims=True).astype(I32)
    place = jnp.where(live, owner * CAP + rank, -1)

    wanted = local + 1
    high = lax.div(wanted, 32)
    low = wanted - high * 32
    asked = jnp.concatenate(
        [
            jnp.where(mine, high.astype(F32), 0.0),
            jnp.where(mine, low.astype(F32), 0.0),
        ],
        axis=0,
    ).astype(BF16)
    lane = jnp.where(live, me * CAP + rank, -1)
    spread = nt(asked, one_hot(iota((places, slots), 0) == lane))
    asks = spread[:n] * 32.0 + spread[n:]
    for p in range(n):
        ask_send[p] = asks[p : p + 1]
    ask_recv[me] = ask_send[me]

    pl.semaphore_wait(barrier, n - 1)

    def copy_to(exchange, d):
        send, recv, ssem, rsem, view = exchange
        peer = lax.rem(me + d, n)
        return pltpu.make_async_remote_copy(
            src_ref=view(send, peer),
            dst_ref=view(recv, me),
            send_sem=ssem.at[peer],
            recv_sem=rsem.at[me],
            device_id={"tm": peer},
            device_id_type=MESH,
        )

    def copy_from(exchange, d):
        send, recv, ssem, rsem, view = exchange
        peer = lax.rem(me - d + n, n)
        return pltpu.make_async_remote_copy(
            src_ref=view(send, peer),
            dst_ref=view(recv, peer),
            send_sem=ssem.at[peer],
            recv_sem=rsem.at[peer],
            device_id={"tm": peer},
            device_id_type=MESH,
        )

    def start(exchange):
        @pl.loop(1, n)
        def _(d):
            copy_to(exchange, d).start()

    def wait_recv(exchange):
        @pl.loop(1, n)
        def _(d):
            copy_from(exchange, d).wait_recv()

    def wait_send(exchange):
        @pl.loop(1, n)
        def _(d):
            copy_to(exchange, d).wait_send()

    def one(ref, index):
        return ref.at[index]

    def span(index):
        return pl.ds(pl.multiple_of(index * CAP, CAP), CAP)

    def rows(ref, index):
        return ref.at[span(index)]

    own = span(me)
    ask = (ask_send, ask_recv, ask_ssem, ask_rsem, one)
    x = (x_send, x_recv, x_ssem, x_rsem, rows)
    p = (p_send, p_recv, p_ssem, p_rsem, rows)

    start(ask)

    row_copy.wait()
    index = iota((1, slots), 1)
    high = lax.div(index, 32)
    fields = iota((CAP, slots), 0)
    fields = jnp.where(
        fields == 0,
        high,
        jnp.where(fields == 1, index - high * 32, jnp.where(fields == 2, row_ref[...] + 1, 0)),
    )
    moved = nt(fields.astype(F32).astype(BF16), one_hot(iota((places, slots), 0) == place))
    slot_row[...] = (moved[0:1] * 32.0 + moved[1:2]).astype(I32)
    slot_copy = pltpu.make_async_copy(slot_row, slot_at, slot_sem)
    slot_copy.start()
    obs_row = moved[2:3].astype(I32)
    obs_column = to_column(obs_row)
    to_obs = one_hot(obs_row == iota((obs_blocks, places), 0) + 1)
    from_obs = one_hot(obs_column == iota((places, obs_blocks), 1) + 1)
    emission_copy.wait()
    total = jnp.zeros((1, places), I32)
    for part in range(PARTS):
        steps = range(part * n // PARTS, (part + 1) * n // PARTS)
        heard = jnp.zeros((1, places), F32)
        for d in steps:
            if d > 0:
                copy_from(ask, d).wait_recv()
        for d in steps:
            heard = heard + ask_recv[lax.rem(me - d + n, n)]
        heard = heard.astype(I32)
        total = total + heard
        picked = nn(one_hot(to_column(heard) == iota((places, panel), 1) + 1), emission[...])
        answers = x_send.at[pl.ds(part * places, places)]
        answers[...] = picked.astype(BF16)
        for d in steps:
            if d > 0:
                copy_to((answers, x_recv, x_ssem, x_rsem, rows), n - d).start()
            else:
                x_recv[own] = answers[own]

    for copy in foot_copies:
        copy.wait()
    observed_copy.wait()
    weight_copy.wait()
    valid_copy.wait()
    slot_copy.wait()

    sub = iota((CAP, width), 0)

    def blocks_of(panel_index):
        first = panel_index * CAP
        indices = [jnp.clip(slot_at[0, first + k], 0, slots - 1) for k in range(CAP)]
        return jnp.concatenate([foot[index] for index in indices], axis=0)

    for d0 in range(0, n, BATCH):
        steps = range(d0, min(d0 + BATCH, n))
        for d in steps:
            if d > 0:
                copy_from(x, n - d).wait_recv()
        for d in steps:
            source = lax.rem(me + d, n)
            product = nt(x_recv[span(source)], blocks_of(source))
            out = jnp.zeros((CAP, width), F32)
            for k in range(CAP):
                out = jnp.where(sub == k, product[:, k * width : (k + 1) * width], out)
            image_rows[span(source)] = out

    rows_value = image_rows[...]
    high, low = split(rows_value)
    image = nn(to_obs, high) + nn(to_obs, low)
    obs_slot = iota((obs_blocks, width), 0) * width + iota((obs_blocks, width), 1)
    misfit = jnp.where(obs_slot < valid_ref[0], weight[...] * (image - observed[...]), 0.0)
    weighted_ref[...] = misfit
    residual[...] = nn(from_obs, misfit.astype(BF16)).astype(BF16)

    for d0 in range(1, n + 1, BATCH):
        steps = range(d0, min(d0 + BATCH, n + 1))
        for d in steps:
            target = lax.rem(me + d, n)
            value = residual[span(target)].astype(F32)
            wide = jnp.concatenate(
                [jnp.where(sub == k, value, 0.0) for k in range(CAP)], axis=1
            ).astype(BF16)
            high, low = split(nn(wide, blocks_of(target)))
            sink = p_send if d < n else p_recv
            sink[span(target), :width] = high
            sink[span(target), width:] = low
        for d in steps:
            if d < n:
                copy_to(p, d).start()
    scatter = one_hot(iota((panel, places), 0) + 1 == total)
    prior_copy.wait()
    wait_send(ask)
    wait_send(x)
    wait_recv(p)
    summed = nn(scatter, p_recv[...])
    gradient_ref[...] = (
        summed[:, :width] + summed[:, width:] + prior[...] * emission[...].astype(F32)
    )
    wait_send(p)


def in_hbm(value):
    return pltpu.with_memory_space_constraint(value, pltpu.HBM)


def on_device(
    footprint,
    block_row,
    block_col,
    block_count,
    observed_count,
    emission,
    observed,
    error_weight,
    prior_precision,
):
    n = lax.axis_size("tm")
    slots, width, _ = footprint.shape
    panel = emission.shape[0]
    obs_blocks = observed.shape[0]
    places = n * CAP
    hbm_spec = pl.BlockSpec(memory_space=pltpu.HBM)
    any_spec = pl.BlockSpec(memory_space=pl.ANY)
    vmem_spec = pl.BlockSpec(memory_space=pltpu.VMEM)
    dma = pltpu.SemaphoreType.DMA
    outs = (
        jax.ShapeDtypeStruct((panel, width), F32),
        jax.ShapeDtypeStruct((obs_blocks, width), F32),
    )
    results = pl.pallas_call(
        functools.partial(kernel, n),
        out_shape=outs,
        in_specs=[hbm_spec] * 9,
        out_specs=(vmem_spec, vmem_spec),
        scratch_shapes=[
            pltpu.VMEM((1, slots), I32),
            pltpu.VMEM((1, slots), I32),
            pltpu.SMEM((1,), I32),
            pltpu.SMEM((1,), I32),
            pltpu.VMEM((slots, width, width), BF16),
            pltpu.VMEM((panel, width), BF16),
            pltpu.VMEM((obs_blocks, width), F32),
            pltpu.VMEM((obs_blocks, width), F32),
            pltpu.VMEM((panel, width), F32),
            pltpu.VMEM((n, 1, places), F32),
            pltpu.VMEM((n, 1, places), F32),
            pltpu.VMEM((PARTS * places, width), BF16),
            pltpu.VMEM((places, width), BF16),
            pltpu.VMEM((places, 2 * width), BF16),
            pltpu.VMEM((places, 2 * width), BF16),
            pltpu.VMEM((1, places), I32),
            pltpu.SMEM((1, places), I32),
            pltpu.VMEM((places, width), F32),
            pltpu.VMEM((places, width), BF16),
            dma((CHUNKS,)),
            dma(()),
            dma((8,)),
            dma((n,)),
            dma((n,)),
            dma((n,)),
            dma((n,)),
            dma((n,)),
            dma((n,)),
        ],
        compiler_params=pltpu.CompilerParams(
            collective_id=0, has_side_effects=True, vmem_limit_bytes=48 * 1024 * 1024
        ),
        cost_estimate=pl.CostEstimate(
            flops=4 * slots * width * width,
            bytes_accessed=footprint.size * 2 + panel * width * 10,
            transcendentals=0,
        ),
    )(
        in_hbm(footprint),
        in_hbm(block_row),
        in_hbm(block_col),
        block_count,
        observed_count,
        in_hbm(emission),
        in_hbm(observed),
        in_hbm(error_weight),
        in_hbm(prior_precision),
    )
    return results


def solution(mesh):
    placed = (
        P(("members", "tm"), None, None),
        P(("members", "tm"), None),
        P(("members", "tm"), None),
        P(("members", "tm")),
        P(("members", "tm")),
        P(("members", "tm"), None),
        P(("members", "tm"), None),
        P(("members", "tm"), None),
        P(("members", "tm"), None),
    )
    return jax.shard_map(
        on_device,
        mesh=mesh,
        in_specs=placed,
        out_specs=(P(("members", "tm"), None), P(("members", "tm"), None)),
        check_vma=False,
    )
```
